32 devices in a mesh: parts: 2 (over y), clus: 4 (over z), sub: 4 (over x, core).
Axes of the slice: x: 2, y: 2, z: 4, core: 2. Of those that a mesh axis runs over, the one named last changes fastest.
Arguments:
- vector: bfloat16 [2, 16, 16384], P(None, None, ('parts', 'clus', 'sub')), parts along dimension 2, may hold values from -6 to 6
- near_blocks: bfloat16 [1536, 2, 128, 128], P(('parts', 'clus', 'sub')), parts along dimension 0, may hold values from -0.15625 to 0.15625
- near_rows: int32 [1536], P(('parts', 'clus', 'sub')), parts along dimension 0, may hold values from 0 to 63, as said below
- near_cols: int32 [1536], P(('parts', 'clus', 'sub')), parts along dimension 0, may hold values from 0 to 63, as said below
- row_basis: bfloat16 [2, 32, 16384], P(None, None, ('parts', 'clus', 'sub')), parts along dimension 2, may hold values from -0.75 to 0.75
- col_basis: bfloat16 [2, 32, 16384], P(None, None, ('parts', 'clus', 'sub')), parts along dimension 2, may hold values from -0.09375 to 0.09375
- couplings: bfloat16 [256, 2, 32, 32], P(('parts', 'clus', 'sub')), parts along dimension 0, may hold values from -0.125 to 0.125
- far_cols: int32 [256], P(('parts', 'clus', 'sub')), parts along dimension 0, may hold values from 0 to 3, as said below
Outputs:
- first_product: bfloat16 [2, 16, 16384], P(None, None, ('parts', 'clus', 'sub')), parts along dimension 2
- second_product: bfloat16 [2, 16, 16384], P(None, None, ('parts', 'clus', 'sub')), parts along dimension 2
The draws below stay inside these ranges and needn't reach their ends.
There are 2 independent parts, one for each index of `parts`. The reference program is written for one: setup_inputs(seed, part) draws one part's arguments, and reference() takes and returns one part's arrays. A program takes and returns all parts, laid end to end along the dimension named above; each array names one. Nothing has to cross between parts.
Inputs may be any that keep to these rules, and one draw needn't show every extreme that they name: `near_rows`: the row leaf of a block lies in the subtree of the clus index that holds the block. `near_cols`: the column leaf of a block lies in its row leaf's subtree or an adjacent subtree, at most 16 leaves from the row leaf. `far_cols`: the column subtree of a pair of subtree s is never s.
All inputs are finite; a program needn't handle non-finite values.
Results may differ from the reference program's by a relative error of at most 0.017.
Values may be sent and summed in bfloat16 or wider, within the bound.
A program may use at most 64 MiB of HBM per device.

```python
import jax
import jax.numpy as jnp
from jax import lax

LEAF = 128
RANK = 32
NRHS = 16
LEAF_DEV = 4
NEAR_DEV = 48
FAR_DEV = 8
SUB_ROWS = 2048
SUB_LEAVES = 16
ROWS = 8192
LEAVES = 64
NEAR_ALL = 768
FAR_ALL = 128
N_CLUS = 4
N_SUB = 4


def near_pairs(key):
    positions = jnp.arange(NEAR_ALL, dtype=jnp.int32)
    subtree = positions // (NEAR_DEV * N_SUB)
    key_a, key_b, key_c = jax.random.split(key, 3)
    first_pick = jax.random.randint(key_a, (NEAR_ALL,), 0, SUB_LEAVES, dtype=jnp.int32)
    second_pick = jax.random.randint(key_b, (NEAR_ALL,), 0, SUB_LEAVES, dtype=jnp.int32)
    row_leaf = subtree * SUB_LEAVES + jnp.minimum(first_pick, second_pick)
    row_leaf = jnp.where(positions == 0, 0, row_leaf)
    row_leaf = jnp.where(positions == NEAR_ALL - 1, LEAVES - 1, row_leaf)
    lower = jnp.maximum(jnp.maximum(subtree - 1, 0) * SUB_LEAVES, row_leaf - SUB_LEAVES)
    upper = jnp.minimum(jnp.minimum(subtree + 2, N_CLUS) * SUB_LEAVES, row_leaf + SUB_LEAVES + 1)
    col_leaf = jax.random.randint(key_c, (NEAR_ALL,), lower, upper, dtype=jnp.int32)
    col_leaf = jnp.where(positions == 0, 0, col_leaf)
    col_leaf = jnp.where(positions == NEAR_ALL - 1, LEAVES - 1, col_leaf)
    return (row_leaf.astype(jnp.int32), col_leaf.astype(jnp.int32))


def draw_near_rows(key, part):
    return near_pairs(key)[0]


def draw_near_cols(key, part):
    return near_pairs(key)[1]


def draw_far_cols(key, part):
    key = jax.random.fold_in(key, 7)
    positions = jnp.arange(FAR_ALL, dtype=jnp.int32)
    subtree = positions // (FAR_DEV * N_SUB)
    offset = jax.random.randint(key, (FAR_ALL,), 0, N_CLUS - 1, dtype=jnp.int32)
    column = (subtree + 1 + offset) % N_CLUS
    forced = positions % (FAR_DEV * N_SUB) == 0
    column = jnp.where(forced, (subtree + N_CLUS - 1) % N_CLUS, column)
    return column.astype(jnp.int32)


def levels(rng, dims, shards, least, top_value):
    factor_of = 1.0
    for dim, shards_of in shards:
        heights = jax.random.uniform(jax.random.fold_in(jax.random.fold_in(rng, 6), dim), (shards_of,), jnp.float32, least / len(shards), top_value / len(shards))
        factor_of = factor_of * jnp.repeat(jnp.exp(heights), dims[dim] // shards_of).reshape((-1,) + (1,) * (len(dims) - 1 - dim))
    return factor_of


def scatter_about(own_key, extent, deviation, limit, cuts=(), held_as=jnp.bfloat16):
    entries = deviation * jax.random.normal(own_key, extent, jnp.float32)
    if cuts:
        entries = entries * levels(own_key, extent, cuts, -0.22, 0.18)
    return jnp.clip(entries, -limit, limit).astype(held_as)


def setup_inputs(seed: int = 0, part: int = 0) -> dict:
    keys = jax.random.split(jax.random.key(seed), 9)
    part_splits = jax.random.split(jax.random.fold_in(keys[8], part), 9)
    return {
        "vector": scatter_about(part_splits[0], (2, NRHS, ROWS), 1.0, 6.0, ((2, 16),)),
        "near_blocks": scatter_about(part_splits[1], (NEAR_ALL, 2, LEAF, LEAF), (LEAF * NEAR_DEV // LEAF_DEV) ** -0.5, 0.15625, ((0, 16),)),
        "near_rows": draw_near_rows(jax.random.fold_in(jax.random.fold_in(keys[8], part), 71), part),
        "near_cols": draw_near_cols(jax.random.fold_in(jax.random.fold_in(keys[8], part), 71), part),
        "row_basis": scatter_about(part_splits[4], (2, RANK, ROWS), (2 * RANK) ** -0.5, 0.75, ((2, 16),)),
        "col_basis": scatter_about(part_splits[5], (2, RANK, ROWS), (2 * SUB_ROWS) ** -0.5, 0.09375, ((2, 16),)),
        "couplings": scatter_about(part_splits[6], (FAR_ALL, 2, RANK, RANK), (2 * RANK * FAR_DEV * N_SUB) ** -0.5, 0.125, ((0, 16),)),
        "far_cols": draw_far_cols(jax.random.fold_in(jax.random.fold_in(keys[8], part), 71), part),
    }


def combine(products):
    return jnp.stack([products[0, 0] - products[1, 1], products[0, 1] + products[1, 0]])


def reference(vector, near_blocks, near_rows, near_cols, row_basis, col_basis, couplings, far_cols):
    devices = N_CLUS * N_SUB
    block_groups = near_blocks.reshape(devices, NEAR_DEV, 2, LEAF, LEAF)
    row_groups = near_rows.reshape(devices, NEAR_DEV)
    col_groups = near_cols.reshape(devices, NEAR_DEV)
    device_ids = jnp.arange(devices, dtype=jnp.int32)
    pair_owner = jnp.arange(FAR_ALL, dtype=jnp.int32) // (FAR_DEV * N_SUB)

    def apply_operator(current):
        leaves = current.astype(jnp.float32).reshape(2, NRHS, LEAVES, LEAF)

        def device_step(total, inputs):
            blocks, rows_here, cols_here, device = inputs
            picked = jnp.take(leaves, cols_here, axis=2)
            products = jnp.einsum("bqrc,pnbc->qpnbr", blocks.astype(jnp.float32), picked)
            contrib = combine(products).transpose(2, 0, 1, 3)
            subtree = device // N_SUB
            local_rows = (rows_here - subtree * SUB_LEAVES).astype(jnp.int32)
            partial_value = jax.ops.segment_sum(contrib, local_rows, num_segments=SUB_LEAVES)
            partial_value = lax.optimization_barrier(partial_value.astype(jnp.bfloat16)).astype(jnp.float32)
            start = (subtree * SUB_LEAVES).astype(jnp.int32)
            before = lax.dynamic_slice_in_dim(total, start, SUB_LEAVES, 0)
            total = lax.dynamic_update_slice_in_dim(total, before + partial_value, start, 0)
            return total, None

        start_total = jnp.zeros((LEAVES, 2, NRHS, LEAF), jnp.float32)
        near_total, _ = lax.scan(device_step, start_total, (block_groups, row_groups, col_groups, device_ids))
        near_part = near_total.transpose(1, 2, 0, 3).reshape(2, NRHS, ROWS)

        basis_cols = col_basis.astype(jnp.float32).reshape(2, RANK, N_CLUS, SUB_ROWS)
        grouped = current.astype(jnp.float32).reshape(2, NRHS, N_CLUS, SUB_ROWS)
        coefficients = combine(jnp.einsum("qktr,pntr->qpntk", basis_cols, grouped))
        coefficients = coefficients.transpose(2, 0, 1, 3).astype(jnp.bfloat16)
        picked_coeff = jnp.take(coefficients, far_cols, axis=0).astype(jnp.float32)
        pair_terms = combine(jnp.einsum("fqkj,fpnj->qpfnk", couplings.astype(jnp.float32), picked_coeff))
        coupled = jax.ops.segment_sum(pair_terms.transpose(1, 0, 2, 3), pair_owner, num_segments=N_CLUS)
        coupled = coupled.astype(jnp.bfloat16).astype(jnp.float32)
        basis_rows = row_basis.astype(jnp.float32).reshape(2, RANK, N_CLUS, SUB_ROWS)
        far_part = combine(jnp.einsum("qktr,tpnk->qpntr", basis_rows, coupled)).reshape(2, NRHS, ROWS)
        return (near_part + far_part).astype(jnp.bfloat16)

    first_product = apply_operator(vector)
    second_product = apply_operator(first_product)
    return first_product, second_product
```

```python
import functools

import jax
import jax.numpy as jnp
from jax import lax
from jax.experimental import pallas as pl
from jax.experimental.pallas import tpu as pltpu
from jax.sharding import PartitionSpec as P

F32 = jnp.float32
BF16 = jnp.bfloat16
NT = (((1,), (1,)), ((), ()))
CHUNKS = 4
STEP = 8


def kernel(
    clus_count, sub_count, leaf_size,
    vec, blocks, rows, cols, rowb, colb, coup, farc,
    out0, out1,
    blk, blk_sem, idx_v, idx_s, idx_sem, wcol, wcoup, xw0, xw1, xrs, xss, fss,
    csend, crecv, crs, css, coef0, coef1, grs, gss,
    dsend, drecv, drs, dss, sums, nown, nsend, nrecv, nrs, nss,
):
    t = lax.axis_index("clus")
    s = lax.axis_index("sub")
    g = s // 2
    c = s - 2 * g
    groups = sub_count // 2
    leaf_dev = vec.shape[2] // leaf_size
    sub_leaves = leaf_dev * sub_count
    rhs = vec.shape[1]
    nb = blk.shape[0]
    part = nb // CHUNKS
    far_dev = coup.shape[0]
    partner = 2 * g + 1 - c

    loads = [
        pltpu.make_async_copy(
            blocks.at[pl.ds(i * part, part)], blk.at[pl.ds(i * part, part)], blk_sem.at[i]
        )
        for i in range(CHUNKS)
    ]
    for load in loads:
        load.start()

    def has(dt):
        return (t > 0) if dt < 0 else (t < clus_count - 1)

    def remote(src, dst, ssem, rsem, tt, ss):
        return pltpu.make_async_remote_copy(
            src_ref=src, dst_ref=dst, send_sem=ssem, recv_sem=rsem,
            device_id={"clus": tt, "sub": ss}, device_id_type=pl.DeviceIdType.MESH,
        )

    barrier = pltpu.get_barrier_semaphore()

    def greet(tt, ss):
        pl.semaphore_signal(
            barrier, inc=1, device_id={"clus": tt, "sub": ss}, device_id_type=pl.DeviceIdType.MESH
        )

    for j in range(1, sub_count):
        greet(t, lax.rem(s + j, sub_count))
    expected = sub_count - 1
    for dt in (-1, 1):
        @pl.when(has(dt))
        def _(dt=dt):
            for j in range(groups):
                greet(t + dt, 2 * lax.rem(g + j, groups) + c)

        expected = expected + jnp.where(has(dt), groups, 0)
    for d in range(2, clus_count):
        for sign in (-1, 1):
            ok = (t - d >= 0) if sign < 0 else (t + d < clus_count)

            @pl.when(ok)
            def _(d=d, sign=sign):
                greet(t + sign * d, s)

            expected = expected + jnp.where(ok, 1, 0)

    i0 = lax.broadcasted_iota(jnp.int32, (nb, nb), 0)
    i1 = lax.broadcasted_iota(jnp.int32, (nb, nb), 1)
    row_l = jnp.clip(rows[...] - t * sub_leaves, 0, sub_leaves - 1)
    col_l = jnp.clip(cols[...] - (t - 1) * sub_leaves, 0, 3 * sub_leaves - 1)
    eye = i0 == i1
    row_c = jnp.sum(jnp.where(eye, row_l, 0), axis=1, keepdims=True)
    col_c = jnp.sum(jnp.where(eye, col_l, 0), axis=1, keepdims=True)
    key_r = row_l * nb + i1
    key_c = row_c * nb + i0
    rank = jnp.sum(jnp.where(key_r < key_c, 1, 0), axis=1, keepdims=True)
    hit = rank == i1
    idx_v[0:1, 0:nb] = jnp.sum(jnp.where(hit, i0, 0), axis=0, keepdims=True)
    idx_v[1:2, 0:nb] = jnp.sum(jnp.where(hit, row_c, 0), axis=0, keepdims=True)
    idx_v[2:3, 0:nb] = jnp.sum(jnp.where(hit, col_c, 0), axis=0, keepdims=True)
    leaf = lax.broadcasted_iota(jnp.int32, (nb, sub_leaves), 1)
    upto = jnp.sum(jnp.where(row_c <= leaf, 1, 0), axis=0, keepdims=True)
    here = jnp.sum(jnp.where(row_c == leaf, 1, 0), axis=0, keepdims=True)
    idx_v[3:4, 0:sub_leaves] = jnp.where(here > 0, upto, 0)
    idx_copy = pltpu.make_async_copy(idx_v, idx_s, idx_sem)
    idx_copy.start()

    wcol[...] = jnp.concatenate(
        [
            jnp.concatenate([colb[0], -colb[1]], axis=1),
            jnp.concatenate([colb[1], colb[0]], axis=1),
        ],
        axis=0,
    )

    def slot(w, ss):
        return pl.ds((w * sub_count + ss) * leaf_dev, leaf_dev)

    own = (sub_count + s) * leaf_dev
    for l in range(leaf_dev):
        for p in range(2):
            xw0[own + l, p] = vec[p, :, l * leaf_size : (l + 1) * leaf_size]
    sums[0] = jnp.zeros(sums.shape[1:], F32)

    pl.semaphore_wait(barrier, expected)

    for prod in range(2):
        x = vec if prod == 0 else out0
        out = out0 if prod == 0 else out1
        xw = (xw0, xw1)[prod]
        coef = (coef0, coef1)[prod]

        def shard_send(dt, j, prod=prod, xw=xw):
            target = partner if (dt == 0 and j == 0) else 2 * lax.rem(g + j, groups) + c
            return remote(
                xw.at[slot(1, s)], xw.at[slot(1 - dt, s)],
                xss.at[prod, dt + 1, j], xrs.at[prod, 1 - dt, s], t + dt, target,
            )

        def forward(w, j, prod=prod, xw=xw):
            ss = 2 * lax.rem(g + j, groups) + c
            return remote(
                xw.at[slot(w, ss)], xw.at[slot(w, ss)],
                fss.at[prod, w, j], xrs.at[prod, w, ss], t, partner,
            )

        def from_partner(w, j, prod=prod, xw=xw):
            ss = 2 * lax.rem(g + j, groups) + 1 - c
            return remote(
                xw.at[slot(w, ss)], xw.at[slot(w, ss)],
                fss.at[prod, w, j], xrs.at[prod, w, ss], t, partner,
            )

        for j in list(range(1, groups)) + [0]:
            for dt in (-1, 1):
                @pl.when(has(dt))
                def _(dt=dt, j=j):
                    shard_send(dt, j).start()
            shard_send(0, j).start()

        lhs = jnp.concatenate([x[0], x[1]], axis=1)
        partial = lax.dot_general(lhs, wcol[...], NT, preferred_element_type=F32)
        csend[prod] = partial

        def coef_send(j, prod=prod):
            return remote(
                csend.at[prod], crecv.at[prod, s], css.at[prod, j], crs.at[prod, s],
                t, lax.rem(s + j, sub_count),
            )

        def coef_recv(j, prod=prod):
            ss = lax.rem(s + j, sub_count)
            return remote(
                csend.at[prod], crecv.at[prod, ss], css.at[prod, j], crs.at[prod, ss], t, ss
            )

        for j in range(1, sub_count):
            coef_send(j).start()
        if prod == 0:
            for f in range(far_dev):
                wcoup[f] = jnp.concatenate(
                    [
                        jnp.concatenate([coup[f, 0], -coup[f, 1]], axis=1),
                        jnp.concatenate([coup[f, 1], coup[f, 0]], axis=1),
                    ],
                    axis=0,
                )
        for j in range(1, sub_count):
            coef_recv(j).wait_recv()
            partial = partial + crecv[prod, lax.rem(s + j, sub_count)]
        coef[t] = partial.astype(BF16)

        def gather_send(d, prod=prod, coef=coef):
            return remote(
                coef.at[t], coef.at[t], gss.at[prod, d], grs.at[prod, t],
                lax.rem(t + d, clus_count), s,
            )

        def gather_recv(d, prod=prod, coef=coef):
            tt = lax.rem(t + d, clus_count)
            return remote(coef.at[tt], coef.at[tt], gss.at[prod, d], grs.at[prod, tt], tt, s)

        for d in range(1, clus_count):
            gather_send(d).start()

        for j in range(groups):
            for dt in (-1, 1):
                @pl.when(has(dt))
                def _(dt=dt, j=j):
                    hop = forward(1 + dt, j)
                    hop.wait_recv()
                    hop.start()
            if j > 0:
                hop = forward(1, j)
                hop.wait_recv()
                hop.start()

        for d in range(1, clus_count):
            gather_recv(d).wait_recv()
        coupled = jnp.zeros(partial.shape, F32)
        for f in range(far_dev):
            coupled = coupled + lax.dot_general(
                coef[farc[f]], wcoup[f], NT, preferred_element_type=F32
            )
        dsend[prod] = coupled

        def coupled_send(j, prod=prod):
            return remote(
                dsend.at[prod], drecv.at[prod, s], dss.at[prod, j], drs.at[prod, s],
                t, lax.rem(s + j, sub_count),
            )

        def coupled_recv(j, prod=prod):
            ss = lax.rem(s + j, sub_count)
            return remote(
                dsend.at[prod], drecv.at[prod, ss], dss.at[prod, j], drs.at[prod, ss], t, ss
            )

        for j in range(1, sub_count):
            coupled_send(j).start()

        if prod == 0:
            idx_copy.wait()
            for load in loads:
                load.wait()
        for j in range(groups):
            for dt in (-1, 1):
                @pl.when(has(dt))
                def _(dt=dt, j=j):
                    from_partner(1 + dt, j).wait_recv()
            from_partner(1, j).wait_recv()

        def body(i, total, xw=xw):
            for u in range(STEP):
                k = i * STEP + u
                a = blk[idx_s[0, k]]
                v = xw[idx_s[2, k]]
                left = jnp.concatenate(
                    [
                        jnp.concatenate([v[0], -v[1]], axis=1),
                        jnp.concatenate([v[1], v[0]], axis=1),
                    ],
                    axis=0,
                )
                term = lax.dot_general(
                    left, jnp.concatenate([a[0], a[1]], axis=1), NT, preferred_element_type=F32
                )
                same = idx_s[1, k] == idx_s[1, jnp.maximum(k - 1, 0)]
                total = jnp.where(same, total, 0.0) + term
                sums[k + 1] = total
            return total

        lax.fori_loop(0, nb // STEP, body, jnp.zeros(sums.shape[1:], F32))

        def near_send(jg, e, prod=prod):
            ss = 2 * lax.rem(g + jg, groups) + lax.rem(c + e, 2)
            return ss, remote(
                nsend.at[prod, ss], nrecv.at[prod, s], nss.at[prod, jg, e], nrs.at[prod, s], t, ss
            )

        def near_recv(jg, e, prod=prod):
            ss = 2 * lax.rem(g + jg, groups) + lax.rem(c + e, 2)
            return ss, remote(
                nsend.at[prod, ss], nrecv.at[prod, ss], nss.at[prod, jg, e], nrs.at[prod, ss], t, ss
            )

        others = [(jg, e) for jg in list(range(1, groups)) + [0] for e in range(2)]
        others.remove((0, 0))
        for jg, e in others:
            ss, copy = near_send(jg, e)
            for l in range(leaf_dev):
                nsend[prod, ss, l] = sums[idx_s[3, ss * leaf_dev + l]].astype(BF16)
            copy.start()

        coupled = dsend[prod]
        for j in range(1, sub_count):
            coupled_recv(j).wait_recv()
            coupled = coupled + drecv[prod, lax.rem(s + j, sub_count)]
        coupled = coupled.astype(BF16)
        rank_size = coupled.shape[1] // 2
        c0, c1 = coupled[:, :rank_size], coupled[:, rank_size:]
        left = jnp.concatenate(
            [jnp.concatenate([c0, -c1], axis=1), jnp.concatenate([c1, c0], axis=1)], axis=0
        )
        right = jnp.concatenate([rowb[0], rowb[1]], axis=0)
        far = jnp.dot(left, right, preferred_element_type=F32)
        for l in range(leaf_dev):
            nown[l] = far[:, l * leaf_size : (l + 1) * leaf_size] + sums[
                idx_s[3, s * leaf_dev + l]
            ].astype(BF16).astype(F32)

        for jg, e in others[::-1]:
            near_recv(jg, e)[1].wait_recv()
        for l in range(leaf_dev):
            total = nown[l]
            for jg, e in others:
                ss = 2 * lax.rem(g + jg, groups) + lax.rem(c + e, 2)
                total = total + nrecv[prod, ss, l].astype(F32)
            total = total.astype(BF16)
            for p in range(2):
                piece = total[p * rhs : (p + 1) * rhs]
                out[p, :, l * leaf_size : (l + 1) * leaf_size] = piece
                if prod == 0:
                    xw1[own + l, p] = piece

    for prod in range(2):
        xw = (xw0, xw1)[prod]
        coef = (coef0, coef1)[prod]

        def sent(src, sem):
            remote(src, src, sem, sem, t, partner).wait_send()

        for j in range(groups):
            for dt in (-1, 1):
                @pl.when(has(dt))
                def _(dt=dt, j=j, prod=prod, xw=xw):
                    sent(xw.at[slot(1, s)], xss.at[prod, dt + 1, j])
                    ss = 2 * lax.rem(g + j, groups) + c
                    sent(xw.at[slot(1 + dt, ss)], fss.at[prod, 1 + dt, j])
            sent(xw.at[slot(1, s)], xss.at[prod, 1, j])
            if j > 0:
                ss = 2 * lax.rem(g + j, groups) + c
                sent(xw.at[slot(1, ss)], fss.at[prod, 1, j])
        for j in range(1, sub_count):
            sent(csend.at[prod], css.at[prod, j])
            sent(dsend.at[prod], dss.at[prod, j])
        for d in range(1, clus_count):
            sent(coef.at[t], gss.at[prod, d])
        for jg in range(groups):
            for e in range(2):
                if (jg, e) != (0, 0):
                    ss = 2 * lax.rem(g + jg, groups) + lax.rem(c + e, 2)
                    sent(nsend.at[prod, ss], nss.at[prod, jg, e])


def per_device(
    vector, near_blocks, near_rows, near_cols, row_basis, col_basis, couplings, far_cols
):
    sub_count = lax.axis_size("sub")
    clus_count = lax.axis_size("clus")
    groups = sub_count // 2
    nb, _, leaf_size, _ = near_blocks.shape
    _, rhs, rows_dev = vector.shape
    leaf_dev = rows_dev // leaf_size
    window = 3 * sub_count * leaf_dev
    rank = row_basis.shape[1]
    far_dev = couplings.shape[0]
    dma = pltpu.SemaphoreType.DMA
    small = (rhs, 2 * rank)
    vmem = pl.BlockSpec(memory_space=pltpu.VMEM)
    smem = pl.BlockSpec(memory_space=pltpu.SMEM)
    return pl.pallas_call(
        functools.partial(kernel, clus_count, sub_count, leaf_size),
        out_shape=(
            jax.ShapeDtypeStruct(vector.shape, BF16),
            jax.ShapeDtypeStruct(vector.shape, BF16),
        ),
        in_specs=[vmem, pl.BlockSpec(memory_space=pl.ANY), vmem, vmem, vmem, vmem, vmem, smem],
        out_specs=(vmem, vmem),
        scratch_shapes=[
            pltpu.VMEM(near_blocks.shape, BF16), dma((CHUNKS,)),
            pltpu.VMEM((8, 128), jnp.int32), pltpu.SMEM((8, 128), jnp.int32), dma(()),
            pltpu.VMEM((2 * rank, 2 * rows_dev), BF16),
            pltpu.VMEM((far_dev, 2 * rank, 2 * rank), BF16),
            pltpu.VMEM((window, 2, rhs, leaf_size), BF16),
            pltpu.VMEM((window, 2, rhs, leaf_size), BF16),
            dma((2, 3, sub_count)), dma((2, 3, groups)), dma((2, 3, groups)),
            pltpu.VMEM((2,) + small, F32), pltpu.VMEM((2, sub_count) + small, F32),
            dma((2, sub_count)), dma((2, sub_count)),
            pltpu.VMEM((clus_count,) + small, BF16), pltpu.VMEM((clus_count,) + small, BF16),
            dma((2, clus_count)), dma((2, clus_count)),
            pltpu.VMEM((2,) + small, F32), pltpu.VMEM((2, sub_count) + small, F32),
            dma((2, sub_count)), dma((2, sub_count)),
            pltpu.VMEM((nb + 1, 2 * rhs, leaf_size), F32),
            pltpu.VMEM((leaf_dev, 2 * rhs, leaf_size), F32),
            pltpu.VMEM((2, sub_count, leaf_dev, 2 * rhs, leaf_size), BF16),
            pltpu.VMEM((2, sub_count, leaf_dev, 2 * rhs, leaf_size), BF16),
            dma((2, sub_count)), dma((2, groups, 2)),
        ],
        compiler_params=pltpu.CompilerParams(
            collective_id=0, has_side_effects=True, vmem_limit_bytes=40 * 1024 * 1024
        ),
        name="operator",
    )(
        vector, near_blocks, near_rows.reshape(1, nb), near_cols.reshape(1, nb),
        row_basis, col_basis, couplings, far_cols,
    )


def solution(mesh):
    in_specs = (
        P(None, None, ("parts", "clus", "sub")),
        P(("parts", "clus", "sub"), None, None, None),
        P(("parts", "clus", "sub")),
        P(("parts", "clus", "sub")),
        P(None, None, ("parts", "clus", "sub")),
        P(None, None, ("parts", "clus", "sub")),
        P(("parts", "clus", "sub"), None, None, None),
        P(("parts", "clus", "sub")),
    )
    out_specs = (P(None, None, ("parts", "clus", "sub")), P(None, None, ("parts", "clus", "sub")))
    return jax.shard_map(
        per_device, mesh=mesh, in_specs=in_specs, out_specs=out_specs, check_vma=False
    )
```

```python
import functools

import jax
import jax.numpy as jnp
from jax import lax
from jax.experimental import pallas as pl
from jax.experimental.pallas import tpu as pltpu
from jax.sharding import PartitionSpec as P

F32 = jnp.float32
BF16 = jnp.bfloat16
NT = (((1,), (1,)), ((), ()))
CHUNKS = 4
STEP = 48


def kernel(
    clus_count, sub_count, leaf_size,
    vec_h, blocks, rows_h, cols_h, rowb_h, colb_h, coup_h, farc_h,
    out0, out1,
    vec, rows, cols, rowb, colb, coup, farc, in_sem,
    blk, blk_sem, idx_v, idx_s, idx_sem, wcol, wcoup, xw0, xw1, xrs, xss, fss,
    csend, crecv, crs, css, coef0, coef1, grs, gss,
    dsend, drecv, drs, dss, sums, nown, nsend, nrecv, nrs, nss,
):
    t = lax.axis_index("clus")
    s = lax.axis_index("sub")
    g = s // 2
    c = s - 2 * g
    groups = sub_count // 2
    leaf_dev = vec.shape[2] // leaf_size
    sub_leaves = leaf_dev * sub_count
    rhs = vec.shape[1]
    nb = blk.shape[0]
    part = nb // CHUNKS
    far_dev = coup.shape[0]
    partner = 2 * g + 1 - c

    vec_in, rows_in, cols_in, farc_in, colb_in, coup_in, rowb_in = [
        pltpu.make_async_copy(source, target, in_sem.at[i])
        for i, (source, target) in enumerate(
            [
                (vec_h, vec), (rows_h, rows), (cols_h, cols), (farc_h, farc),
                (colb_h, colb), (coup_h, coup), (rowb_h, rowb),
            ]
        )
    ]
    for load in (vec_in, rows_in, cols_in, farc_in, colb_in, coup_in, rowb_in):
        load.start()
    loads = [
        pltpu.make_async_copy(
            blocks.at[pl.ds(i * part, part)], blk.at[pl.ds(i * part, part)], blk_sem.at[i]
        )
        for i in range(CHUNKS)
    ]
    for load in loads:
        load.start()

    def has(dt):
        return (t > 0) if dt < 0 else (t < clus_count - 1)

    def remote(src, dst, ssem, rsem, tt, ss):
        return pltpu.make_async_remote_copy(
            src_ref=src, dst_ref=dst, send_sem=ssem, recv_sem=rsem,
            device_id={"clus": tt, "sub": ss}, device_id_type=pl.DeviceIdType.MESH,
        )

    barrier = pltpu.get_barrier_semaphore()

    def greet(tt, ss):
        pl.semaphore_signal(
            barrier, inc=1, device_id={"clus": tt, "sub": ss}, device_id_type=pl.DeviceIdType.MESH
        )

    for j in range(1, sub_count):
        greet(t, lax.rem(s + j, sub_count))
    expected = sub_count - 1
    for dt in (-1, 1):
        @pl.when(has(dt))
        def _(dt=dt):
            for j in range(groups):
                greet(t + dt, 2 * lax.rem(g + j, groups) + c)

        expected = expected + jnp.where(has(dt), groups, 0)
    for d in range(2, clus_count):
        for sign in (-1, 1):
            ok = (t - d >= 0) if sign < 0 else (t + d < clus_count)

            @pl.when(ok)
            def _(d=d, sign=sign):
                greet(t + sign * d, s)

            expected = expected + jnp.where(ok, 1, 0)

    def slot(w, ss):
        return pl.ds((w * sub_count + ss) * leaf_dev, leaf_dev)

    own = (sub_count + s) * leaf_dev
    vec_in.wait()
    for l in range(leaf_dev):
        for p in range(2):
            xw0[own + l, p] = vec[p, :, l * leaf_size : (l + 1) * leaf_size]
    sums[0] = jnp.zeros(sums.shape[1:], F32)
    for load in (rows_in, cols_in, farc_in):
        load.wait()

    i0 = lax.broadcasted_iota(jnp.int32, (nb, nb), 0)
    i1 = lax.broadcasted_iota(jnp.int32, (nb, nb), 1)
    row_l = jnp.clip(rows[...] - t * sub_leaves, 0, sub_leaves - 1)
    col_l = jnp.clip(cols[...] - (t - 1) * sub_leaves, 0, 3 * sub_leaves - 1)
    eye = i0 == i1
    row_c = jnp.sum(jnp.where(eye, row_l, 0), axis=1, keepdims=True)
    col_c = jnp.sum(jnp.where(eye, col_l, 0), axis=1, keepdims=True)
    key_r = row_l * nb + i1
    key_c = row_c * nb + i0
    rank = jnp.sum(jnp.where(key_r < key_c, 1, 0), axis=1, keepdims=True)
    hit = rank == i1
    idx_v[0:1, 0:nb] = jnp.sum(jnp.where(hit, i0, 0), axis=0, keepdims=True)
    idx_v[1:2, 0:nb] = jnp.sum(jnp.where(hit, row_c, 0), axis=0, keepdims=True)
    idx_v[2:3, 0:nb] = jnp.sum(jnp.where(hit, col_c, 0), axis=0, keepdims=True)
    leaf = lax.broadcasted_iota(jnp.int32, (nb, sub_leaves), 1)
    upto = jnp.sum(jnp.where(row_c <= leaf, 1, 0), axis=0, keepdims=True)
    here = jnp.sum(jnp.where(row_c == leaf, 1, 0), axis=0, keepdims=True)
    idx_v[3:4, 0:sub_leaves] = jnp.where(here > 0, upto, 0)
    idx_v[4:5, 0:far_dev] = farc[...]
    idx_copy = pltpu.make_async_copy(idx_v, idx_s, idx_sem)
    idx_copy.start()

    colb_in.wait()
    wcol[...] = jnp.concatenate(
        [
            jnp.concatenate([colb[0], -colb[1]], axis=1),
            jnp.concatenate([colb[1], colb[0]], axis=1),
        ],
        axis=0,
    )

    pl.semaphore_wait(barrier, expected)

    for prod in range(2):
        x = vec if prod == 0 else out0
        out = out0 if prod == 0 else out1
        xw = (xw0, xw1)[prod]
        coef = (coef0, coef1)[prod]

        def shard_send(dt, j, prod=prod, xw=xw):
            target = partner if (dt == 0 and j == 0) else 2 * lax.rem(g + j, groups) + c
            return remote(
                xw.at[slot(1, s)], xw.at[slot(1 - dt, s)],
                xss.at[prod, dt + 1, j], xrs.at[prod, 1 - dt, s], t + dt, target,
            )

        def forward(w, j, prod=prod, xw=xw):
            ss = 2 * lax.rem(g + j, groups) + c
            return remote(
                xw.at[slot(w, ss)], xw.at[slot(w, ss)],
                fss.at[prod, w, j], xrs.at[prod, w, ss], t, partner,
            )

        def from_partner(w, j, prod=prod, xw=xw):
            ss = 2 * lax.rem(g + j, groups) + 1 - c
            return remote(
                xw.at[slot(w, ss)], xw.at[slot(w, ss)],
                fss.at[prod, w, j], xrs.at[prod, w, ss], t, partner,
            )

        for j in list(range(1, groups)) + [0]:
            for dt in (-1, 1):
                @pl.when(has(dt))
                def _(dt=dt, j=j):
                    shard_send(dt, j).start()
            shard_send(0, j).start()

        lhs = jnp.concatenate([x[0], x[1]], axis=1)
        partial = lax.dot_general(lhs, wcol[...], NT, preferred_element_type=F32)
        csend[prod] = partial

        def coef_send(j, prod=prod):
            return remote(
                csend.at[prod], crecv.at[prod, s], css.at[prod, j], crs.at[prod, s],
                t, lax.rem(s + j, sub_count),
            )

        def coef_recv(j, prod=prod):
            ss = lax.rem(s + j, sub_count)
            return remote(
                csend.at[prod], crecv.at[prod, ss], css.at[prod, j], crs.at[prod, ss], t, ss
            )

        for j in range(1, sub_count):
            coef_send(j).start()
        if prod == 0:
            coup_in.wait()
            rowb_in.wait()
            idx_copy.wait()
            for f in range(far_dev):
                wcoup[f] = jnp.concatenate(
                    [
                        jnp.concatenate([coup[f, 0], -coup[f, 1]], axis=1),
                        jnp.concatenate([coup[f, 1], coup[f, 0]], axis=1),
                    ],
                    axis=0,
                )
        for j in range(1, sub_count):
            coef_recv(j).wait_recv()
            partial = partial + crecv[prod, lax.rem(s + j, sub_count)]
        coef[t] = partial.astype(BF16)

        def gather_send(d, prod=prod, coef=coef):
            return remote(
                coef.at[t], coef.at[t], gss.at[prod, d], grs.at[prod, t],
                lax.rem(t + d, clus_count), s,
            )

        def gather_recv(d, prod=prod, coef=coef):
            tt = lax.rem(t + d, clus_count)
            return remote(coef.at[tt], coef.at[tt], gss.at[prod, d], grs.at[prod, tt], tt, s)

        for d in range(1, clus_count):
            gather_send(d).start()

        for j in range(groups):
            for dt in (-1, 1):
                @pl.when(has(dt))
                def _(dt=dt, j=j):
                    hop = forward(1 + dt, j)
                    hop.wait_recv()
                    hop.start()
            if j > 0:
                hop = forward(1, j)
                hop.wait_recv()
                hop.start()

        for d in range(1, clus_count):
            gather_recv(d).wait_recv()
        coupled = jnp.zeros(partial.shape, F32)
        for f in range(far_dev):
            coupled = coupled + lax.dot_general(
                coef[idx_s[4, f]], wcoup[f], NT, preferred_element_type=F32
            )
        dsend[prod] = coupled

        def coupled_send(j, prod=prod):
            return remote(
                dsend.at[prod], drecv.at[prod, s], dss.at[prod, j], drs.at[prod, s],
                t, lax.rem(s + j, sub_count),
            )

        def coupled_recv(j, prod=prod):
            ss = lax.rem(s + j, sub_count)
            return remote(
                dsend.at[prod], drecv.at[prod, ss], dss.at[prod, j], drs.at[prod, ss], t, ss
            )

        for j in range(1, sub_count):
            coupled_send(j).start()

        if prod == 0:
            for load in loads:
                load.wait()
        for j in range(groups):
            for dt in (-1, 1):
                @pl.when(has(dt))
                def _(dt=dt, j=j):
                    from_partner(1 + dt, j).wait_recv()
            from_partner(1, j).wait_recv()

        def body(i, total, xw=xw):
            for u in range(STEP):
                k = i * STEP + u
                a = blk[idx_s[0, k]]
                v = xw[idx_s[2, k]]
                left = jnp.concatenate(
                    [
                        jnp.concatenate([v[0], -v[1]], axis=1),
                        jnp.concatenate([v[1], v[0]], axis=1),
                    ],
                    axis=0,
                )
                term = lax.dot_general(
                    left, jnp.concatenate([a[0], a[1]], axis=1), NT, preferred_element_type=F32
                )
                same = idx_s[1, k] == idx_s[1, jnp.maximum(k - 1, 0)]
                total = jnp.where(same, total, 0.0) + term
                sums[k + 1] = total
            return total

        lax.fori_loop(0, nb // STEP, body, jnp.zeros(sums.shape[1:], F32))

        def near_send(jg, e, prod=prod):
            ss = 2 * lax.rem(g + jg, groups) + lax.rem(c + e, 2)
            return ss, remote(
                nsend.at[prod, ss], nrecv.at[prod, s], nss.at[prod, jg, e], nrs.at[prod, s], t, ss
            )

        def near_recv(jg, e, prod=prod):
            ss = 2 * lax.rem(g + jg, groups) + lax.rem(c + e, 2)
            return ss, remote(
                nsend.at[prod, ss], nrecv.at[prod, ss], nss.at[prod, jg, e], nrs.at[prod, ss], t, ss
            )

        others = [(jg, e) for jg in list(range(1, groups)) + [0] for e in range(2)]
        others.remove((0, 0))
        for jg, e in others:
            ss, copy = near_send(jg, e)
            for l in range(leaf_dev):
                nsend[prod, ss, l] = sums[idx_s[3, ss * leaf_dev + l]].astype(BF16)
            copy.start()

        coupled = dsend[prod]
        for j in range(1, sub_count):
            coupled_recv(j).wait_recv()
            coupled = coupled + drecv[prod, lax.rem(s + j, sub_count)]
        coupled = coupled.astype(BF16)
        rank_size = coupled.shape[1] // 2
        c0, c1 = coupled[:, :rank_size], coupled[:, rank_size:]
        left = jnp.concatenate(
            [jnp.concatenate([c0, -c1], axis=1), jnp.concatenate([c1, c0], axis=1)], axis=0
        )
        right = jnp.concatenate([rowb[0], rowb[1]], axis=0)
        far = jnp.dot(left, right, preferred_element_type=F32)
        for l in range(leaf_dev):
            nown[l] = far[:, l * leaf_size : (l + 1) * leaf_size] + sums[
                idx_s[3, s * leaf_dev + l]
            ].astype(BF16).astype(F32)

        for jg, e in others[::-1]:
            near_recv(jg, e)[1].wait_recv()
        for l in range(leaf_dev):
            total = nown[l]
            for jg, e in others:
                ss = 2 * lax.rem(g + jg, groups) + lax.rem(c + e, 2)
                total = total + nrecv[prod, ss, l].astype(F32)
            total = total.astype(BF16)
            for p in range(2):
                piece = total[p * rhs : (p + 1) * rhs]
                out[p, :, l * leaf_size : (l + 1) * leaf_size] = piece
                if prod == 0:
                    xw1[own + l, p] = piece

    for prod in range(2):
        xw = (xw0, xw1)[prod]
        coef = (coef0, coef1)[prod]

        def sent(src, sem):
            remote(src, src, sem, sem, t, partner).wait_send()

        for j in range(groups):
            for dt in (-1, 1):
                @pl.when(has(dt))
                def _(dt=dt, j=j, prod=prod, xw=xw):
                    sent(xw.at[slot(1, s)], xss.at[prod, dt + 1, j])
                    ss = 2 * lax.rem(g + j, groups) + c
                    sent(xw.at[slot(1 + dt, ss)], fss.at[prod, 1 + dt, j])
            sent(xw.at[slot(1, s)], xss.at[prod, 1, j])
            if j > 0:
                ss = 2 * lax.rem(g + j, groups) + c
                sent(xw.at[slot(1, ss)], fss.at[prod, 1, j])
        for j in range(1, sub_count):
            sent(csend.at[prod], css.at[prod, j])
            sent(dsend.at[prod], dss.at[prod, j])
        for d in range(1, clus_count):
            sent(coef.at[t], gss.at[prod, d])
        for jg in range(groups):
            for e in range(2):
                if (jg, e) != (0, 0):
                    ss = 2 * lax.rem(g + jg, groups) + lax.rem(c + e, 2)
                    sent(nsend.at[prod, ss], nss.at[prod, jg, e])


def per_device(
    vector, near_blocks, near_rows, near_cols, row_basis, col_basis, couplings, far_cols
):
    sub_count = lax.axis_size("sub")
    clus_count = lax.axis_size("clus")
    groups = sub_count // 2
    nb, _, leaf_size, _ = near_blocks.shape
    _, rhs, rows_dev = vector.shape
    leaf_dev = rows_dev // leaf_size
    window = 3 * sub_count * leaf_dev
    rank = row_basis.shape[1]
    far_dev = couplings.shape[0]
    dma = pltpu.SemaphoreType.DMA
    small = (rhs, 2 * rank)
    vmem = pl.BlockSpec(memory_space=pltpu.VMEM)
    return pl.pallas_call(
        functools.partial(kernel, clus_count, sub_count, leaf_size),
        out_shape=(
            jax.ShapeDtypeStruct(vector.shape, BF16),
            jax.ShapeDtypeStruct(vector.shape, BF16),
        ),
        in_specs=[pl.BlockSpec(memory_space=pl.ANY)] * 8,
        out_specs=(vmem, vmem),
        scratch_shapes=[
            pltpu.VMEM(vector.shape, BF16), pltpu.VMEM((1, nb), jnp.int32),
            pltpu.VMEM((1, nb), jnp.int32), pltpu.VMEM(row_basis.shape, BF16),
            pltpu.VMEM(col_basis.shape, BF16), pltpu.VMEM(couplings.shape, BF16),
            pltpu.VMEM((1, far_dev), jnp.int32), dma((7,)),
            pltpu.VMEM(near_blocks.shape, BF16), dma((CHUNKS,)),
            pltpu.VMEM((8, 128), jnp.int32), pltpu.SMEM((8, 128), jnp.int32), dma(()),
            pltpu.VMEM((2 * rank, 2 * rows_dev), BF16),
            pltpu.VMEM((far_dev, 2 * rank, 2 * rank), BF16),
            pltpu.VMEM((window, 2, rhs, leaf_size), BF16),
            pltpu.VMEM((window, 2, rhs, leaf_size), BF16),
            dma((2, 3, sub_count)), dma((2, 3, groups)), dma((2, 3, groups)),
            pltpu.VMEM((2,) + small, F32), pltpu.VMEM((2, sub_count) + small, F32),
            dma((2, sub_count)), dma((2, sub_count)),
            pltpu.VMEM((clus_count,) + small, BF16), pltpu.VMEM((clus_count,) + small, BF16),
            dma((2, clus_count)), dma((2, clus_count)),
            pltpu.VMEM((2,) + small, F32), pltpu.VMEM((2, sub_count) + small, F32),
            dma((2, sub_count)), dma((2, sub_count)),
            pltpu.VMEM((nb + 1, 2 * rhs, leaf_size), F32),
            pltpu.VMEM((leaf_dev, 2 * rhs, leaf_size), F32),
            pltpu.VMEM((2, sub_count, leaf_dev, 2 * rhs, leaf_size), BF16),
            pltpu.VMEM((2, sub_count, leaf_dev, 2 * rhs, leaf_size), BF16),
            dma((2, sub_count)), dma((2, groups, 2)),
        ],
        compiler_params=pltpu.CompilerParams(
            collective_id=0, has_side_effects=True, vmem_limit_bytes=60 * 1024 * 1024
        ),
        name="operator",
    )(
        vector, near_blocks, near_rows.reshape(1, nb), near_cols.reshape(1, nb),
        row_basis, col_basis, couplings, far_cols.reshape(1, far_dev),
    )


def solution(mesh):
    in_specs = (
        P(None, None, ("parts", "clus", "sub")),
        P(("parts", "clus", "sub"), None, None, None),
        P(("parts", "clus", "sub")),
        P(("parts", "clus", "sub")),
        P(None, None, ("parts", "clus", "sub")),
        P(None, None, ("parts", "clus", "sub")),
        P(("parts", "clus", "sub"), None, None, None),
        P(("parts", "clus", "sub")),
    )
    out_specs = (P(None, None, ("parts", "clus", "sub")), P(None, None, ("parts", "clus", "sub")))
    return jax.shard_map(
        per_device, mesh=mesh, in_specs=in_specs, out_specs=out_specs, check_vma=False
    )
```

```python
import functools

import jax
import jax.numpy as jnp
from jax import lax
from jax.experimental import pallas as pl
from jax.experimental.pallas import tpu as pltpu
from jax.sharding import PartitionSpec as P

F32 = jnp.float32
BF16 = jnp.bfloat16
NT = (((1,), (1,)), ((), ()))
CHUNKS = 4
STEP = 48


def kernel(
    clus_count, sub_count, leaf_size,
    vec_h, blocks, rows_h, cols_h, rowb_h, colb_h, coup_h, farc_h,
    out0, out1,
    vec, rows, cols, rowb, colb, coup, farc, in_sem,
    blk, blk_sem, idx_v, idx_s, idx_sem, wcol, wcoup, xw0, xw1, xrs, xss, fss,
    crecv, crs, css, coef0, coef1,
    dsend, drecv, drs, dss, sums, nown, nsend, nrecv, nrs, nss,
):
    t = lax.axis_index("clus")
    s = lax.axis_index("sub")
    g = s // 2
    c = s - 2 * g
    groups = sub_count // 2
    leaf_dev = vec.shape[2] // leaf_size
    sub_leaves = leaf_dev * sub_count
    rhs = vec.shape[1]
    nb = blk.shape[0]
    part = nb // CHUNKS
    far_dev = coup.shape[0]
    rank_size = coup.shape[2]
    half = 2 * rank_size
    partner = 2 * g + 1 - c

    vec_in, rows_in, cols_in, farc_in, colb_in, coup_in, rowb_in = [
        pltpu.make_async_copy(source, target, in_sem.at[i])
        for i, (source, target) in enumerate(
            [
                (vec_h, vec), (rows_h, rows), (cols_h, cols), (farc_h, farc),
                (colb_h, colb), (coup_h, coup), (rowb_h, rowb),
            ]
        )
    ]
    for load in (vec_in, rows_in, cols_in, farc_in, colb_in, coup_in, rowb_in):
        load.start()
    loads = [
        pltpu.make_async_copy(
            blocks.at[pl.ds(i * part, part)], blk.at[pl.ds(i * part, part)], blk_sem.at[i]
        )
        for i in range(CHUNKS)
    ]
    for load in loads:
        load.start()

    def has(dt):
        return (t > 0) if dt < 0 else (t < clus_count - 1)

    def remote(src, dst, ssem, rsem, tt, ss):
        return pltpu.make_async_remote_copy(
            src_ref=src, dst_ref=dst, send_sem=ssem, recv_sem=rsem,
            device_id={"clus": tt, "sub": ss}, device_id_type=pl.DeviceIdType.MESH,
        )

    mates = clus_count * sub_count - 1

    def mate(i):
        d, j = i // sub_count, i % sub_count
        return lax.rem(t + d, clus_count), lax.rem(s + j, sub_count)

    def each(act):
        if mates < 32:
            for i in range(1, mates + 1):
                act(i)
        else:
            lax.fori_loop(1, mates + 1, lambda i, state: (act(i), state)[1], 0)

    barrier = pltpu.get_barrier_semaphore()

    def greet(tt, ss):
        pl.semaphore_signal(
            barrier, inc=1, device_id={"clus": tt, "sub": ss}, device_id_type=pl.DeviceIdType.MESH
        )

    each(lambda i: greet(*mate(i)))

    def slot(w, ss):
        return pl.ds((w * sub_count + ss) * leaf_dev, leaf_dev)

    own = (sub_count + s) * leaf_dev
    vec_in.wait()
    for l in range(leaf_dev):
        for p in range(2):
            xw0[own + l, p] = vec[p, :, l * leaf_size : (l + 1) * leaf_size]
    sums[0] = jnp.zeros(sums.shape[1:], F32)
    for load in (rows_in, cols_in, farc_in):
        load.wait()

    i0 = lax.broadcasted_iota(jnp.int32, (nb, nb), 0)
    i1 = lax.broadcasted_iota(jnp.int32, (nb, nb), 1)
    row_l = jnp.clip(rows[...] - t * sub_leaves, 0, sub_leaves - 1)
    col_l = jnp.clip(cols[...] - (t - 1) * sub_leaves, 0, 3 * sub_leaves - 1)
    eye = i0 == i1
    row_c = jnp.sum(jnp.where(eye, row_l, 0), axis=1, keepdims=True)
    col_c = jnp.sum(jnp.where(eye, col_l, 0), axis=1, keepdims=True)
    key_r = row_l * nb + i1
    key_c = row_c * nb + i0
    rank = jnp.sum(jnp.where(key_r < key_c, 1, 0), axis=1, keepdims=True)
    hit = rank == i1
    idx_v[0:1, 0:nb] = jnp.sum(jnp.where(hit, i0, 0), axis=0, keepdims=True)
    idx_v[1:2, 0:nb] = jnp.sum(jnp.where(hit, row_c, 0), axis=0, keepdims=True)
    idx_v[2:3, 0:nb] = jnp.sum(jnp.where(hit, col_c, 0), axis=0, keepdims=True)
    leaf = lax.broadcasted_iota(jnp.int32, (nb, sub_leaves), 1)
    upto = jnp.sum(jnp.where(row_c <= leaf, 1, 0), axis=0, keepdims=True)
    here = jnp.sum(jnp.where(row_c == leaf, 1, 0), axis=0, keepdims=True)
    idx_v[3:4, 0:sub_leaves] = jnp.where(here > 0, upto, 0)
    idx_v[4:5, 0:far_dev] = farc[...]
    idx_copy = pltpu.make_async_copy(idx_v, idx_s, idx_sem)
    idx_copy.start()

    colb_in.wait()
    wcol[...] = jnp.concatenate(
        [
            jnp.concatenate([colb[0], -colb[1]], axis=1),
            jnp.concatenate([colb[1], colb[0]], axis=1),
            jnp.zeros((wcol.shape[0] - 2 * rank_size, wcol.shape[1]), BF16),
        ],
        axis=0,
    )

    pl.semaphore_wait(barrier, mates)

    for prod in range(2):
        x = vec if prod == 0 else out0
        out = out0 if prod == 0 else out1
        xw = (xw0, xw1)[prod]
        coef = (coef0, coef1)[prod]

        def shard_send(dt, j, prod=prod, xw=xw):
            target = partner if (dt == 0 and j == 0) else 2 * lax.rem(g + j, groups) + c
            return remote(
                xw.at[slot(1, s)], xw.at[slot(1 - dt, s)],
                xss.at[prod, dt + 1, j], xrs.at[prod, 1 - dt, s], t + dt, target,
            )

        def forward(w, j, prod=prod, xw=xw):
            ss = 2 * lax.rem(g + j, groups) + c
            return remote(
                xw.at[slot(w, ss)], xw.at[slot(w, ss)],
                fss.at[prod, w, j], xrs.at[prod, w, ss], t, partner,
            )

        def from_partner(w, j, prod=prod, xw=xw):
            ss = 2 * lax.rem(g + j, groups) + 1 - c
            return remote(
                xw.at[slot(w, ss)], xw.at[slot(w, ss)],
                fss.at[prod, w, j], xrs.at[prod, w, ss], t, partner,
            )

        for j in list(range(1, groups)) + [0]:
            for dt in (-1, 1):
                @pl.when(has(dt))
                def _(dt=dt, j=j):
                    shard_send(dt, j).start()
            shard_send(0, j).start()

        lhs = jnp.concatenate([x[0], x[1]], axis=1)
        partial = lax.dot_general(lhs, wcol[...], NT, preferred_element_type=F32)
        me = t * sub_count + s
        crecv[prod, me] = jnp.concatenate(
            [partial[: rhs // 2, :half], partial[rhs // 2 :, :half]], axis=1
        )

        def coef_send(i, prod=prod, me=me):
            tt, ss = mate(i)
            return remote(
                crecv.at[prod, me], crecv.at[prod, me], css.at[prod, i], crs.at[prod, me], tt, ss
            )

        def coef_recv(i, prod=prod):
            tt, ss = mate(i)
            here = tt * sub_count + ss
            return remote(
                crecv.at[prod, here], crecv.at[prod, here], css.at[prod, i], crs.at[prod, here],
                tt, ss,
            )

        each(lambda i: coef_send(i).start())
        if prod == 0:
            coup_in.wait()
            rowb_in.wait()
            idx_copy.wait()
            wcoup[...] = jnp.zeros(wcoup.shape, BF16)
            coef0[...] = jnp.zeros(coef0.shape, BF16)
            coef1[...] = jnp.zeros(coef1.shape, BF16)
            for f in range(far_dev):
                wcoup[f, : 2 * rank_size, : 2 * rank_size] = jnp.concatenate(
                    [
                        jnp.concatenate([coup[f, 0], -coup[f, 1]], axis=1),
                        jnp.concatenate([coup[f, 1], coup[f, 0]], axis=1),
                    ],
                    axis=0,
                )
        for j in range(groups):
            for dt in (-1, 1):
                @pl.when(has(dt))
                def _(dt=dt, j=j):
                    hop = forward(1 + dt, j)
                    hop.wait_recv()
                    hop.start()
            if j > 0:
                hop = forward(1, j)
                hop.wait_recv()
                hop.start()

        each(lambda i: coef_recv(i).wait_recv())
        for tt in range(clus_count):
            packed = crecv[prod, tt * sub_count]
            for ss in range(1, sub_count):
                packed = packed + crecv[prod, tt * sub_count + ss]
            coef[tt, :, :half] = jnp.concatenate(
                [packed[:, :half], packed[:, half:]], axis=0
            ).astype(BF16)
        coupled = jnp.zeros(partial.shape, F32)
        for f in range(far_dev):
            coupled = coupled + lax.dot_general(
                coef[idx_s[4, f]], wcoup[f], NT, preferred_element_type=F32
            )
        dsend[prod] = coupled

        def coupled_send(j, prod=prod):
            return remote(
                dsend.at[prod], drecv.at[prod, s], dss.at[prod, j], drs.at[prod, s],
                t, lax.rem(s + j, sub_count),
            )

        def coupled_recv(j, prod=prod):
            ss = lax.rem(s + j, sub_count)
            return remote(
                dsend.at[prod], drecv.at[prod, ss], dss.at[prod, j], drs.at[prod, ss], t, ss
            )

        for j in range(1, sub_count):
            coupled_send(j).start()

        if prod == 0:
            for load in loads:
                load.wait()
        for j in range(groups):
            for dt in (-1, 1):
                @pl.when(has(dt))
                def _(dt=dt, j=j):
                    from_partner(1 + dt, j).wait_recv()
            from_partner(1, j).wait_recv()

        def body(i, total, xw=xw):
            for u in range(STEP):
                k = i * STEP + u
                a = blk[idx_s[0, k]]
                v = xw[idx_s[2, k]]
                left = jnp.concatenate(
                    [
                        jnp.concatenate([v[0], -v[1]], axis=1),
                        jnp.concatenate([v[1], v[0]], axis=1),
                    ],
                    axis=0,
                )
                term = lax.dot_general(
                    left, jnp.concatenate([a[0], a[1]], axis=1), NT, preferred_element_type=F32
                )
                same = idx_s[1, k] == idx_s[1, jnp.maximum(k - 1, 0)]
                total = jnp.where(same, total, 0.0) + term
                sums[k + 1] = total
            return total

        lax.fori_loop(0, nb // STEP, body, jnp.zeros(sums.shape[1:], F32))

        def near_send(jg, e, prod=prod):
            ss = 2 * lax.rem(g + jg, groups) + lax.rem(c + e, 2)
            return ss, remote(
                nsend.at[prod, ss], nrecv.at[prod, s], nss.at[prod, jg, e], nrs.at[prod, s], t, ss
            )

        def near_recv(jg, e, prod=prod):
            ss = 2 * lax.rem(g + jg, groups) + lax.rem(c + e, 2)
            return ss, remote(
                nsend.at[prod, ss], nrecv.at[prod, ss], nss.at[prod, jg, e], nrs.at[prod, ss], t, ss
            )

        others = [(jg, e) for jg in list(range(1, groups)) + [0] for e in range(2)]
        others.remove((0, 0))
        for jg, e in others:
            ss, copy = near_send(jg, e)
            for l in range(leaf_dev):
                nsend[prod, ss, l] = sums[idx_s[3, ss * leaf_dev + l]].astype(BF16)
            copy.start()

        coupled = dsend[prod]
        for j in range(1, sub_count):
            coupled_recv(j).wait_recv()
            coupled = coupled + drecv[prod, lax.rem(s + j, sub_count)]
        coupled = coupled.astype(BF16)
        c0, c1 = coupled[:, :rank_size], coupled[:, rank_size : 2 * rank_size]
        left = jnp.concatenate(
            [jnp.concatenate([c0, -c1], axis=1), jnp.concatenate([c1, c0], axis=1)], axis=0
        )
        right = jnp.concatenate([rowb[0], rowb[1]], axis=0)
        far = jnp.dot(left, right, preferred_element_type=F32)
        for l in range(leaf_dev):
            nown[l] = far[:, l * leaf_size : (l + 1) * leaf_size] + sums[
                idx_s[3, s * leaf_dev + l]
            ].astype(BF16).astype(F32)

        for jg, e in others[::-1]:
            near_recv(jg, e)[1].wait_recv()
        for l in range(leaf_dev):
            total = nown[l]
            for jg, e in others:
                ss = 2 * lax.rem(g + jg, groups) + lax.rem(c + e, 2)
                total = total + nrecv[prod, ss, l].astype(F32)
            total = total.astype(BF16)
            for p in range(2):
                piece = total[p * rhs : (p + 1) * rhs]
                out[p, :, l * leaf_size : (l + 1) * leaf_size] = piece
                if prod == 0:
                    xw1[own + l, p] = piece

    for prod in range(2):
        xw = (xw0, xw1)[prod]

        def sent(src, sem):
            remote(src, src, sem, sem, t, partner).wait_send()

        for j in range(groups):
            for dt in (-1, 1):
                @pl.when(has(dt))
                def _(dt=dt, j=j, prod=prod, xw=xw):
                    sent(xw.at[slot(1, s)], xss.at[prod, dt + 1, j])
                    ss = 2 * lax.rem(g + j, groups) + c
                    sent(xw.at[slot(1 + dt, ss)], fss.at[prod, 1 + dt, j])
            sent(xw.at[slot(1, s)], xss.at[prod, 1, j])
            if j > 0:
                ss = 2 * lax.rem(g + j, groups) + c
                sent(xw.at[slot(1, ss)], fss.at[prod, 1, j])
        for j in range(1, sub_count):
            sent(dsend.at[prod], dss.at[prod, j])
        each(lambda i, prod=prod: sent(crecv.at[prod, t * sub_count + s], css.at[prod, i]))
        for jg in range(groups):
            for e in range(2):
                if (jg, e) != (0, 0):
                    ss = 2 * lax.rem(g + jg, groups) + lax.rem(c + e, 2)
                    sent(nsend.at[prod, ss], nss.at[prod, jg, e])


def per_device(
    vector, near_blocks, near_rows, near_cols, row_basis, col_basis, couplings, far_cols
):
    sub_count = lax.axis_size("sub")
    clus_count = lax.axis_size("clus")
    groups = sub_count // 2
    nb, _, leaf_size, _ = near_blocks.shape
    _, rhs, rows_dev = vector.shape
    leaf_dev = rows_dev // leaf_size
    window = 3 * sub_count * leaf_dev
    rank = row_basis.shape[1]
    far_dev = couplings.shape[0]
    dma = pltpu.SemaphoreType.DMA
    width = -(-2 * rank // 128) * 128
    small = (rhs, width)
    vmem = pl.BlockSpec(memory_space=pltpu.VMEM)
    return pl.pallas_call(
        functools.partial(kernel, clus_count, sub_count, leaf_size),
        out_shape=(
            pltpu.VMEM(vector.shape, BF16),
            pltpu.VMEM(vector.shape, BF16),
        ),
        in_specs=[pl.BlockSpec(memory_space=pl.ANY)] * 8,
        out_specs=(vmem, vmem),
        scratch_shapes=[
            pltpu.VMEM(vector.shape, BF16), pltpu.VMEM((1, nb), jnp.int32),
            pltpu.VMEM((1, nb), jnp.int32), pltpu.VMEM(row_basis.shape, BF16),
            pltpu.VMEM(col_basis.shape, BF16), pltpu.VMEM(couplings.shape, BF16),
            pltpu.VMEM((1, far_dev), jnp.int32), dma((7,)),
            pltpu.VMEM(near_blocks.shape, BF16), dma((CHUNKS,)),
            pltpu.VMEM((8, 128), jnp.int32), pltpu.SMEM((8, 128), jnp.int32), dma(()),
            pltpu.VMEM((width, 2 * rows_dev), BF16),
            pltpu.VMEM((far_dev, width, width), BF16),
            pltpu.VMEM((window, 2, rhs, leaf_size), BF16),
            pltpu.VMEM((window, 2, rhs, leaf_size), BF16),
            dma((2, 3, sub_count)), dma((2, 3, groups)), dma((2, 3, groups)),
            pltpu.VMEM((2, clus_count * sub_count, rhs // 2, 4 * rank), F32),
            dma((2, clus_count * sub_count)), dma((2, clus_count * sub_count)),
            pltpu.VMEM((clus_count,) + small, BF16), pltpu.VMEM((clus_count,) + small, BF16),
            pltpu.VMEM((2,) + small, F32), pltpu.VMEM((2, sub_count) + small, F32),
            dma((2, sub_count)), dma((2, sub_count)),
            pltpu.VMEM((nb + 1, 2 * rhs, leaf_size), F32),
            pltpu.VMEM((leaf_dev, 2 * rhs, leaf_size), F32),
            pltpu.VMEM((2, sub_count, leaf_dev, 2 * rhs, leaf_size), BF16),
            pltpu.VMEM((2, sub_count, leaf_dev, 2 * rhs, leaf_size), BF16),
            dma((2, sub_count)), dma((2, groups, 2)),
        ],
        compiler_params=pltpu.CompilerParams(
            collective_id=0, has_side_effects=True, vmem_limit_bytes=60 * 1024 * 1024
        ),
        name="operator",
    )(
        vector, near_blocks, near_rows.reshape(1, nb), near_cols.reshape(1, nb),
        row_basis, col_basis, couplings, far_cols.reshape(1, far_dev),
    )


def solution(mesh):
    in_specs = (
        P(None, None, ("parts", "clus", "sub")),
        P(("parts", "clus", "sub"), None, None, None),
        P(("parts", "clus", "sub")),
        P(("parts", "clus", "sub")),
        P(None, None, ("parts", "clus", "sub")),
        P(None, None, ("parts", "clus", "sub")),
        P(("parts", "clus", "sub"), None, None, None),
        P(("parts", "clus", "sub")),
    )
    out_specs = (P(None, None, ("parts", "clus", "sub")), P(None, None, ("parts", "clus", "sub")))
    return jax.shard_map(
        per_device, mesh=mesh, in_specs=in_specs, out_specs=out_specs, check_vma=False
    )
```
